32 devices in a mesh: phase: 2 (over x), ctx: 16 (over z, y, core).
Axes of the slice: x: 2, y: 2, z: 4, core: 2. Of those that a mesh axis runs over, the one named last changes fastest.
Arguments:
- embed: bfloat16 [2048, 4096], P('ctx'), may hold values from -6 to 6
- gains: float32 [2, 4096], P('phase'), may hold values from 0.1 to 1.9
- keys: bfloat16 [2, 2048, 1024], P('phase', 'ctx'), may hold values from -512 to 512
- values: bfloat16 [2, 2048, 1024], P('phase', 'ctx'), may hold values from -6 to 6
- block_order: int32 [16], replicated, may hold values from 0 to 15, each once
- block_doc: int32 [16], replicated, may hold values from 0 to 3, never falling along the last dimension, each value on 1 to 8 neighbouring positions
Outputs:
- phase_output: bfloat16 [2, 2048, 4096], P('phase', 'ctx')
The draws below stay inside these ranges and needn't reach their ends.
Inputs may be any that keep to these rules, and one draw needn't show every extreme that they name: Storage block b of every token-indexed array holds the sequence's block block_order[b]. `block_doc`: documents are numbered in sequence order and never fall; each covers 1 to 8 whole blocks, one exactly 8.
All inputs are finite; a program needn't handle non-finite values.
Results may differ from the reference program's by a relative error of at most 0.0063.
Values may be sent and summed in bfloat16 or wider, within the bound.
A program may use at most 128 MiB of HBM per device.

```python
import math
import jax
import jax.numpy as jnp
import numpy as np
from jax import lax

D = 4096
HEADS = 32
KVH = 8
HDIM = 128
BLOCK = 128
PHASES = 2
TOKENS = 2048
NBLK = 16
DOCS = 4
DOCSPAN = 8
KVW = 1024


def embed_field(key):
    normal_part = jnp.clip(jax.random.normal(jax.random.fold_in(key, 11), (TOKENS, D), jnp.float32), -6.0, 6.0)
    return normal_part


def draw_embed(key, part):
    return embed_field(key).astype(jnp.bfloat16)


def draw_keys(key, part):
    base_keys = jax.random.normal(jax.random.fold_in(key, 12), (PHASES, TOKENS, KVH, HDIM), jnp.float32)
    base_keys = jnp.clip(base_keys * 1.5, -9.0, 9.0)
    return base_keys.reshape(PHASES, TOKENS, KVH * HDIM).astype(jnp.bfloat16)


def levels(rng, dims, shards, least, high):
    level, own = 1.0, jax.random.fold_in(rng, 6)
    for axis_at, parts in shards:
        steps = jnp.exp(jax.random.uniform(jax.random.fold_in(own, axis_at), (parts,), jnp.float32, least / len(shards), high / len(shards)))
        level = level * jnp.repeat(steps, dims[axis_at] // parts).reshape([-1 if axis == axis_at else 1 for axis in range(len(dims))])
    return level


def split_up(amount, total, bound, lean):
    weights = [(1 << 20) // math.isqrt(standing ** lean) + 1 for standing in range(2, amount + 1)]
    rest, holding = total - bound - (amount - 1), [1] * (amount - 1)
    while rest > 0:
        candidates = [i for i in range(amount - 1) if holding[i] < bound]
        mass, left = sum([weights[i] for i in candidates]), rest
        for i in candidates:
            addition = min(bound - holding[i], max(1, left * weights[i] // mass), rest)
            holding[i] = holding[i] + addition
            rest = rest - addition
    return np.array([bound] + holding)


def uneven(own_key, number_of, total, reach, lean):
    if number_of == 2:
        one = jax.random.randint(own_key, (), max(1, total - reach), min(reach, total - 1) + 1)
        return jnp.stack([one, total - one])
    sizes = jnp.asarray(split_up(number_of, total, reach, lean), jnp.int32)
    twos = (number_of - 1) // 2
    source_of, receiver = sizes[1:1 + 2 * twos:2], sizes[2:2 + 2 * twos:2]
    margin = jnp.minimum(source_of - 1, reach - receiver)
    shifted = jax.random.randint(jax.random.fold_in(own_key, 1), (twos,), 0, 1 << 20) % (margin + 1)
    sizes = sizes.at[1:1 + 2 * twos:2].set(source_of - shifted).at[2:2 + 2 * twos:2].set(receiver + shifted)
    return sizes[jax.random.permutation(jax.random.fold_in(own_key, 2), number_of)]


def centred(key, extent, width, most, shards=(), held_as=jnp.bfloat16):
    loudness = levels(key, extent, shards, -0.22, 0.18) if shards else 1.0
    array = jax.random.normal(key, extent, jnp.float32) * width * loudness
    return jnp.minimum(jnp.maximum(array, -most), most).astype(held_as)


def setup_inputs(seed: int = 0) -> dict:
    splits = jax.random.split(jax.random.key(seed), 7)
    return {
        "embed": draw_embed(jax.random.fold_in(splits[6], 71), 0),
        "gains": jnp.clip(1.0 + 0.18 * jax.random.normal(splits[1], (PHASES, D), jnp.float32), 0.1, 1.9),
        "keys": draw_keys(jax.random.fold_in(splits[6], 71), 0),
        "values": centred(splits[3], (PHASES, TOKENS, KVW), 1.0, 6.0, ((0, 2), (1, 16))),
        "block_order": jax.random.permutation(splits[4], NBLK).astype(jnp.int32),
        "block_doc": jnp.searchsorted(jnp.cumsum(uneven(splits[5], DOCS, NBLK, DOCSPAN, 2)), jnp.arange(NBLK), side="right").astype(jnp.int32),
    }


def attend_block(queries, keys_full, values_full, query_pos, query_doc, key_pos, key_doc):
    grouped = queries.astype(jnp.float32).reshape(-1, KVH, HEADS // KVH, HDIM)
    scores = jnp.einsum('rkgd,tkd->rkgt', grouped, keys_full) / math.sqrt(HDIM)
    visible = (key_doc[None, :] == query_doc[:, None]) & (key_pos[None, :] <= query_pos[:, None])
    visible = visible[:, None, None, :]
    masked = jnp.where(visible, scores, -1e+30)
    row_max = lax.optimization_barrier(jnp.max(masked, axis=3, keepdims=True))
    expo = jnp.where(visible, jnp.exp(masked - row_max), 0.0)
    rounded = lax.optimization_barrier(expo.astype(jnp.bfloat16))
    weights = rounded.astype(jnp.float32)
    numer = jnp.einsum('rkgt,tkd->rkgd', weights, values_full)
    return (numer / lax.optimization_barrier(jnp.sum(expo, axis=3))[..., None]).reshape(-1, D)

def reference(embed, gains, keys, values, block_order, block_doc):
    offsets = jnp.arange(BLOCK, dtype=jnp.int32)
    all_pos = (block_order[:, None].astype(jnp.int32) * BLOCK + offsets[None, :]).reshape(TOKENS)
    all_doc = jnp.repeat(block_doc[block_order], BLOCK).astype(jnp.int32)
    hidden = embed
    outputs = []
    for layer_index in range(PHASES):
        wide = hidden.astype(jnp.float32)
        norm_scale = lax.rsqrt(lax.optimization_barrier(jnp.mean(wide * wide, axis=1, keepdims=True)) + 1e-05)
        queries = (wide * norm_scale * gains[layer_index].astype(jnp.float32)).astype(jnp.bfloat16)
        keys_full = keys[layer_index].astype(jnp.float32).reshape(TOKENS, KVH, HDIM)
        values_full = values[layer_index].astype(jnp.float32).reshape(TOKENS, KVH, HDIM)
        query_blocks = queries.reshape(NBLK, BLOCK, D)
        pos_blocks = all_pos.reshape(NBLK, BLOCK)
        doc_blocks = all_doc.reshape(NBLK, BLOCK)

        def one_block(item):
            return attend_block(item[0], keys_full, values_full, item[1], item[2], all_pos, all_doc)
        attended = lax.map(one_block, (query_blocks, pos_blocks, doc_blocks)).reshape(TOKENS, D)
        attended = lax.optimization_barrier(attended.astype(jnp.bfloat16))
        hidden = (wide + attended.astype(jnp.float32)).astype(jnp.bfloat16)
        outputs.append(hidden)
    return jnp.stack(outputs)
```

```python
import functools
import math

import jax
import jax.numpy as jnp
from jax import lax
from jax.experimental import pallas as pl
from jax.experimental.pallas import tpu as pltpu
from jax.sharding import PartitionSpec as P

HEADS = 32
KVH = 8
HDIM = 128
REP = HEADS // KVH
QW = REP * HDIM
NEG = -1e30
MESH = pl.DeviceIdType.MESH


def kernel(
    layers, ctx, block,
    order_ref, doc_ref, embed_ref, gains_ref, keys_ref, values_ref,
    out_ref,
    kv, hbuf, gbuf, obuf, qbuf, mbuf, lbuf, acc, ss_send, ss_recv,
    loc_sem, kv_send, kv_recv, e_send, e_recv, g_send, g_recv,
    s_send, s_recv, z_send, z_recv, o_send, o_recv,
):
    split = KVH // layers
    groups = ctx // split
    p = lax.axis_index("phase")
    c = lax.axis_index("ctx")
    g = lax.rem(c, split)
    z = lax.div(c, split)
    k = p * split + g
    width = embed_ref.shape[1]

    def device_of(head, group):
        return (lax.div(head, split), group * split + lax.rem(head, split))

    def peer(i):
        return lax.rem(k + i, KVH)

    barrier = pltpu.get_barrier_semaphore()
    for i in range(1, KVH):
        pl.semaphore_signal(barrier, inc=1, device_id=device_of(peer(i), z), device_id_type=MESH)

    @pl.when(z > 0)
    def _():
        pl.semaphore_signal(barrier, inc=1, device_id=(p, c - split), device_id_type=MESH)

    @pl.when(z < groups - 1)
    def _():
        pl.semaphore_signal(barrier, inc=1, device_id=(p, c + split), device_id_type=MESH)

    count = KVH - 1 + (z > 0).astype(jnp.int32) + (z < groups - 1).astype(jnp.int32)
    pl.semaphore_wait(barrier, count)

    def cols(head, size):
        return pl.ds(pl.multiple_of(head * size, size), size)

    def remote(src, dst, send, recv, device):
        return pltpu.make_async_remote_copy(
            src_ref=src, dst_ref=dst, send_sem=send, recv_sem=recv,
            device_id=device, device_id_type=MESH,
        )

    def kv_copy(i, which):
        source = (keys_ref, values_ref)[which]
        return remote(
            source.at[0, :, cols(peer(i), HDIM)], kv.at[p, z, g, which],
            kv_send.at[i, which], kv_recv.at[p, g, which], device_of(peer(i), z),
        )

    def kv_arrive(layer, b, which):
        spot = kv.at[layer, z, b, which]
        return remote(spot, spot, kv_send.at[0, which], kv_recv.at[layer, b, which], (p, c))

    def e_copy(i):
        other = lax.rem(g + i, split)
        return remote(
            embed_ref.at[:, cols(p * split + other, QW)], hbuf.at[g],
            e_send.at[i], e_recv.at[g], (p, z * split + other),
        )

    def g_copy(i):
        other = lax.rem(p + i, layers)
        return remote(
            gains_ref.at[:, cols(other * split + g, QW)], gbuf.at[p],
            g_send.at[i], g_recv.at[p], (other, c),
        )

    locals_ = [
        pltpu.make_async_copy(keys_ref.at[0, :, cols(k, HDIM)], kv.at[p, z, g, 0], loc_sem.at[0]),
        pltpu.make_async_copy(values_ref.at[0, :, cols(k, HDIM)], kv.at[p, z, g, 1], loc_sem.at[1]),
        pltpu.make_async_copy(embed_ref.at[:, cols(k, QW)], hbuf.at[g], loc_sem.at[2]),
        pltpu.make_async_copy(gains_ref.at[:, cols(k, QW)], gbuf.at[p], loc_sem.at[3]),
    ]
    for copy in locals_:
        copy.start()
    for i in range(1, KVH):
        kv_copy(i, 0).start()
        kv_copy(i, 1).start()
    for i in range(1, split):
        e_copy(i).start()
    for i in range(1, layers):
        g_copy(i).start()
    for copy in locals_:
        copy.wait()

    def z_copy(layer, src, b, up):
        spot = kv.at[layer, src, b]
        step = split if up else -split
        return remote(
            spot, spot, z_send.at[layer, src, int(up), b], z_recv.at[layer, src, b], (p, c + step)
        )

    def wait_chunk(layer, b):
        @pl.when(jnp.logical_not((p == layer) & (g == b)))
        def _():
            kv_arrive(layer, b, 0).wait_recv()
            kv_arrive(layer, b, 1).wait_recv()

    def send_chunk(layer, src, b, up):
        @pl.when(z < groups - 1 if up else z > 0)
        def _():
            z_copy(layer, src, b, up).start()

    for i in range(split):
        b = lax.rem(g + i, split)
        wait_chunk(0, b)
        send_chunk(0, z, b, True)
        send_chunk(0, z, b, False)

    for i in range(1, split):
        b = lax.rem(g + i, split)
        remote(hbuf.at[b], hbuf.at[b], e_send.at[0], e_recv.at[b], (p, c)).wait_recv()
    for i in range(1, layers):
        other = lax.rem(p + i, layers)
        remote(gbuf.at[other], gbuf.at[other], g_send.at[0], g_recv.at[other], (p, c)).wait_recv()

    lane = lax.broadcasted_iota(jnp.int32, (block, 128), 1)
    diff = lane - lax.broadcasted_iota(jnp.int32, (block, 128), 0)
    factor = math.log2(math.e) / math.sqrt(HDIM)

    def s_copy(layer, i):
        return remote(
            ss_send.at[layer], ss_recv.at[layer, k],
            s_send.at[layer, i], s_recv.at[layer, k], device_of(peer(i), z),
        )

    def make_queries(layer):
        def hidden(j):
            return (hbuf[j] if layer == 0 else obuf[layer - 1, j]).astype(jnp.float32)

        partial = jnp.zeros((block, 128), jnp.float32)
        for j in range(split):
            wide = hidden(j)
            partial = jnp.where(lane == j, jnp.sum(wide * wide, axis=1, keepdims=True), partial)
        turned = partial.T[:8]
        ss_send[layer] = turned
        ss_recv[layer, k] = turned
        for i in range(1, KVH):
            s_copy(layer, i).start()
        for i in range(1, KVH):
            other = peer(i)
            spot = ss_recv.at[layer, other]
            remote(spot, spot, s_send.at[layer, 0], s_recv.at[layer, other], (p, c)).wait_recv()
        total = jnp.sum(ss_recv[layer], axis=0)
        scale = lax.rsqrt(total * (1.0 / width) + 1e-05)
        scale = jnp.concatenate([scale] * (block // 8), axis=0).T
        for j in range(split):
            queries = (hidden(j) * scale[:, j:j + 1] * gbuf[layer]).astype(jnp.bfloat16)
            for i in range(REP):
                qbuf[j, i * block:(i + 1) * block, :] = queries[:, i * HDIM:(i + 1) * HDIM]

    def attend(layer, src, first):
        key_tile = kv[layer, src, :, 0].reshape(split * block, HDIM)
        value_tile = kv[layer, src, :, 1].reshape(split * block, HDIM)

        def rows(j, carry):
            scores = lax.dot_general(
                qbuf[j], key_tile, (((1,), (1,)), ((), ())), preferred_element_type=jnp.float32
            )
            own = order_ref[z * split + j]
            own_doc = doc_ref[own]
            parts = []
            for b in range(split):
                other = order_ref[src * split + b]
                limit = jnp.where(doc_ref[other] == own_doc, (own - other) * block, -(1 << 24))
                bias = jnp.where(diff <= limit, 0.0, NEG)
                part = scores[:, b * block:(b + 1) * block].reshape(REP, block, block)
                parts.append((part * factor + bias[None]).reshape(REP * block, block))
            top = functools.reduce(jnp.maximum, parts)
            top = jnp.max(top, axis=1, keepdims=True)
            if not first:
                old = mbuf[j]
                top = jnp.maximum(old, top)
            else:
                top = jnp.broadcast_to(top, (REP * block, 128))
            expo = [jnp.exp2(part - top) for part in parts]
            added = functools.reduce(jnp.add, expo)
            weights = jnp.concatenate([e.astype(jnp.bfloat16) for e in expo], axis=1)
            product = jnp.dot(weights, value_tile, preferred_element_type=jnp.float32)
            mbuf[j] = top
            if first:
                lbuf[j] = added
                acc[j] = product
            else:
                shrink = jnp.exp2(old - top)
                lbuf[j] = lbuf[j] * shrink + added
                acc[j] = acc[j] * shrink + product
            return carry

        lax.fori_loop(0, split, rows, 0)

    def o_copy(layer, j):
        return remote(
            obuf.at[layer, j], out_ref.at[0, :, cols(k, QW)],
            o_send.at[layer, j], o_recv.at[k], (layer, z * split + j),
        )

    def o_local(layer, j):
        return pltpu.make_async_copy(
            obuf.at[layer, j], out_ref.at[0, :, cols(k, QW)], o_send.at[layer, j]
        )

    def finish(layer):
        for j in range(split):
            wide = (hbuf[j] if layer == 0 else obuf[layer - 1, j]).astype(jnp.float32)
            total = jnp.sum(lbuf[j], axis=1, keepdims=True)
            attended = (acc[j] / total).astype(jnp.bfloat16).astype(jnp.float32)
            for i in range(REP):
                span = slice(i * HDIM, (i + 1) * HDIM)
                obuf[layer, j, :, span] = (
                    wide[:, span] + attended[i * block:(i + 1) * block]
                ).astype(jnp.bfloat16)
            mine = (p == layer) & (g == j)

            @pl.when(mine)
            def _():
                o_local(layer, j).start()

            @pl.when(jnp.logical_not(mine))
            def _():
                o_copy(layer, j).start()

    def send_next(layer, t):
        if layer + 1 == layers:
            return

        @pl.when(z == t)
        def _():
            for b in range(split):
                send_chunk(layer + 1, z, b, True)

        @pl.when(groups - 1 - z == t)
        def _():
            for b in range(split):
                send_chunk(layer + 1, z, b, False)

    for layer in range(layers):
        make_queries(layer)
        attend(layer, z, True)
        if layer == 0:
            for later in range(1, layers):
                for b in range(split):
                    wait_chunk(later, b)
        send_next(layer, 0)

        def step(t, carry):
            below, above = z - t, z + t

            @pl.when(below >= 0)
            def _():
                for b in range(split):
                    z_copy(layer, below, b, True).wait_recv()
                    send_chunk(layer, below, b, True)

            @pl.when(above < groups)
            def _():
                for b in range(split):
                    z_copy(layer, above, b, False).wait_recv()
                    send_chunk(layer, above, b, False)

            send_next(layer, t)

            @pl.when(below >= 0)
            def _():
                attend(layer, below, False)

            @pl.when(above < groups)
            def _():
                attend(layer, above, False)

            return carry

        lax.fori_loop(1, groups, step, 0)
        finish(layer)

    for i in range(1, KVH):
        kv_copy(i, 0).wait_send()
        kv_copy(i, 1).wait_send()
    for i in range(1, split):
        e_copy(i).wait_send()
    for i in range(1, layers):
        g_copy(i).wait_send()
    for layer in range(layers):
        for i in range(1, KVH):
            s_copy(layer, i).wait_send()

        def drain(src, carry):
            @pl.when((src <= z) & (z < groups - 1))
            def _():
                for b in range(split):
                    z_copy(layer, src, b, True).wait_send()

            @pl.when((src >= z) & (z > 0))
            def _():
                for b in range(split):
                    z_copy(layer, src, b, False).wait_send()

            return carry

        lax.fori_loop(0, groups, drain, 0)
        for j in range(split):
            mine = (p == layer) & (g == j)

            @pl.when(mine)
            def _():
                o_local(layer, j).wait()

            @pl.when(jnp.logical_not(mine))
            def _():
                o_copy(layer, j).wait_send()

    for i in range(1, KVH):
        other = peer(i)
        spot = out_ref.at[0, :, cols(other, QW)]
        remote(spot, spot, o_send.at[0, 0], o_recv.at[other], (p, c)).wait_recv()


def body(layers, ctx, embed, gains, keys, values, block_order, block_doc):
    block, width = embed.shape
    split = KVH // layers
    groups = ctx // split
    dma = pltpu.SemaphoreType.DMA
    smem = pl.BlockSpec(memory_space=pltpu.SMEM)
    anywhere = pl.BlockSpec(memory_space=pl.ANY)
    rows = REP * block
    return pl.pallas_call(
        functools.partial(kernel, layers, ctx, block),
        out_shape=jax.ShapeDtypeStruct((1, block, width), jnp.bfloat16),
        in_specs=[smem, smem] + [anywhere] * 4,
        out_specs=anywhere,
        scratch_shapes=[
            pltpu.VMEM((layers, groups, split, 2, block, HDIM), jnp.bfloat16),
            pltpu.VMEM((split, block, QW), jnp.bfloat16),
            pltpu.VMEM((layers, 1, QW), jnp.float32),
            pltpu.VMEM((layers, split, block, QW), jnp.bfloat16),
            pltpu.VMEM((split, rows, HDIM), jnp.bfloat16),
            pltpu.VMEM((split, rows, 128), jnp.float32),
            pltpu.VMEM((split, rows, 128), jnp.float32),
            pltpu.VMEM((split, rows, HDIM), jnp.float32),
            pltpu.VMEM((layers, 8, 128), jnp.float32),
            pltpu.VMEM((layers, KVH, 8, 128), jnp.float32),
            dma((4,)),
            dma((KVH, 2)),
            dma((layers, split, 2)),
            dma((split,)),
            dma((split,)),
            dma((layers,)),
            dma((layers,)),
            dma((layers, KVH)),
            dma((layers, KVH)),
            dma((layers, groups, 2, split)),
            dma((layers, groups, split)),
            dma((layers, split)),
            dma((KVH,)),
        ],
        compiler_params=pltpu.CompilerParams(
            collective_id=0, has_side_effects=True, vmem_limit_bytes=48 * 1024 * 1024
        ),
    )(block_order, block_doc, embed, gains, keys, values)


def solution(mesh):
    placed = (
        P("ctx", None),
        P("phase", None),
        P("phase", "ctx", None),
        P("phase", "ctx", None),
        P(),
        P(),
    )
    run = functools.partial(body, mesh.shape["phase"], mesh.shape["ctx"])
    return jax.shard_map(
        run, mesh=mesh, in_specs=placed, out_specs=P("phase", "ctx", None), check_vma=False
    )
```

```python
import functools
import math

import jax
import jax.numpy as jnp
from jax import lax
from jax.experimental import pallas as pl
from jax.experimental.pallas import tpu as pltpu
from jax.sharding import PartitionSpec as P

HEADS = 32
KVH = 8
HDIM = 128
REP = HEADS // KVH
QW = REP * HDIM
NEG = -1e30
MESH = pl.DeviceIdType.MESH


def kernel(
    layers, ctx, block,
    order_ref, doc_ref, embed_ref, gains_ref, keys_ref, values_ref,
    out_ref,
    kv, hbuf, gbuf, obuf, qbuf, mbuf, lbuf, acc, ss_send, ss_recv, kst, est, rbuf,
    loc_sem, kv_send, kv_recv, e_send, e_recv, g_send, g_recv,
    s_send, s_recv, z_send, z_recv, o_send, o_recv, st_sem, e_st_sem, r_sem,
):
    split = KVH // layers
    groups = ctx // split
    p = lax.axis_index("phase")
    c = lax.axis_index("ctx")
    g = lax.rem(c, split)
    z = lax.div(c, split)
    k = p * split + g
    width = embed_ref.shape[1]

    def device_of(head, group):
        return (lax.div(head, split), group * split + lax.rem(head, split))

    def peer(i):
        return lax.rem(k + i, KVH)

    barrier = pltpu.get_barrier_semaphore()
    for i in range(1, KVH):
        pl.semaphore_signal(barrier, inc=1, device_id=device_of(peer(i), z), device_id_type=MESH)

    @pl.when(z > 0)
    def _():
        pl.semaphore_signal(barrier, inc=1, device_id=(p, c - split), device_id_type=MESH)

    @pl.when(z < groups - 1)
    def _():
        pl.semaphore_signal(barrier, inc=1, device_id=(p, c + split), device_id_type=MESH)

    count = KVH - 1 + (z > 0).astype(jnp.int32) + (z < groups - 1).astype(jnp.int32)
    pl.semaphore_wait(barrier, count)

    def cols(head, size):
        return pl.ds(pl.multiple_of(head * size, size), size)

    def remote(src, dst, send, recv, device):
        return pltpu.make_async_remote_copy(
            src_ref=src, dst_ref=dst, send_sem=send, recv_sem=recv,
            device_id=device, device_id_type=MESH,
        )

    def kv_stage(i, which):
        source = (keys_ref, values_ref)[which]
        return pltpu.make_async_copy(
            source.at[0, :, cols(peer(i), HDIM)], kst.at[i, which], st_sem.at[i, which]
        )

    def kv_copy(i):
        return remote(
            kst.at[i], kv.at[p, z, g], kv_send.at[i], kv_recv.at[p, g], device_of(peer(i), z)
        )

    def kv_arrive(layer, b):
        spot = kv.at[layer, z, b]
        return remote(spot, spot, kv_send.at[0], kv_recv.at[layer, b], (p, c))

    def e_stage(i):
        other = lax.rem(g + i, split)
        return pltpu.make_async_copy(
            embed_ref.at[:, cols(p * split + other, QW)], est.at[i], e_st_sem.at[i]
        )

    def e_copy(i):
        other = lax.rem(g + i, split)
        return remote(est.at[i], hbuf.at[g], e_send.at[i], e_recv.at[g], (p, z * split + other))

    def g_copy(i):
        other = lax.rem(p + i, layers)
        return remote(
            gains_ref.at[:, cols(other * split + g, QW)], gbuf.at[p],
            g_send.at[i], g_recv.at[p], (other, c),
        )

    locals_ = [
        pltpu.make_async_copy(keys_ref.at[0, :, cols(k, HDIM)], kv.at[p, z, g, 0], loc_sem.at[0]),
        pltpu.make_async_copy(values_ref.at[0, :, cols(k, HDIM)], kv.at[p, z, g, 1], loc_sem.at[1]),
        pltpu.make_async_copy(embed_ref.at[:, cols(k, QW)], hbuf.at[g], loc_sem.at[2]),
        pltpu.make_async_copy(gains_ref.at[:, cols(k, QW)], gbuf.at[p], loc_sem.at[3]),
    ]
    for copy in locals_:
        copy.start()
    for i in range(1, KVH):
        kv_stage(i, 0).start()
        kv_stage(i, 1).start()
    for i in range(1, split):
        e_stage(i).start()
    for i in range(1, KVH):
        kv_stage(i, 0).wait()
        kv_stage(i, 1).wait()
        kv_copy(i).start()
    for i in range(1, split):
        e_stage(i).wait()
        e_copy(i).start()
    for i in range(1, layers):
        g_copy(i).start()
    for copy in locals_:
        copy.wait()

    def z_copy(layer, src, b, up):
        spot = kv.at[layer, src, b]
        step = split if up else -split
        return remote(
            spot, spot, z_send.at[layer, src, int(up), b], z_recv.at[layer, src, b], (p, c + step)
        )

    def wait_chunk(layer, b):
        @pl.when(jnp.logical_not((p == layer) & (g == b)))
        def _():
            kv_arrive(layer, b).wait_recv()

    def send_chunk(layer, src, b, up):
        @pl.when(z < groups - 1 if up else z > 0)
        def _():
            z_copy(layer, src, b, up).start()

    for i in range(split):
        b = lax.rem(g + i, split)
        wait_chunk(0, b)
        send_chunk(0, z, b, True)
        send_chunk(0, z, b, False)

    for i in range(1, split):
        b = lax.rem(g + i, split)
        remote(hbuf.at[b], hbuf.at[b], e_send.at[0], e_recv.at[b], (p, c)).wait_recv()
    for i in range(1, layers):
        other = lax.rem(p + i, layers)
        remote(gbuf.at[other], gbuf.at[other], g_send.at[0], g_recv.at[other], (p, c)).wait_recv()

    lane = lax.broadcasted_iota(jnp.int32, (block, 128), 1)
    diff = lane - lax.broadcasted_iota(jnp.int32, (block, 128), 0)
    factor = math.log2(math.e) / math.sqrt(HDIM)

    def s_copy(layer, i):
        return remote(
            ss_send.at[layer], ss_recv.at[layer, k],
            s_send.at[layer, i], s_recv.at[layer, k], device_of(peer(i), z),
        )

    def make_queries(layer):
        def hidden(j):
            return (hbuf[j] if layer == 0 else obuf[layer - 1, j]).astype(jnp.float32)

        partial = jnp.zeros((block, 128), jnp.float32)
        for j in range(split):
            wide = hidden(j)
            partial = jnp.where(lane == j, jnp.sum(wide * wide, axis=1, keepdims=True), partial)
        turned = partial.T[:8]
        ss_send[layer] = turned
        ss_recv[layer, k] = turned
        for i in range(1, KVH):
            s_copy(layer, i).start()
        for i in range(1, KVH):
            other = peer(i)
            spot = ss_recv.at[layer, other]
            remote(spot, spot, s_send.at[layer, 0], s_recv.at[layer, other], (p, c)).wait_recv()
        total = jnp.sum(ss_recv[layer], axis=0)
        scale = lax.rsqrt(total * (1.0 / width) + 1e-05)
        scale = jnp.concatenate([scale] * (block // 8), axis=0).T
        for j in range(split):
            queries = (hidden(j) * scale[:, j:j + 1] * gbuf[layer]).astype(jnp.bfloat16)
            for i in range(REP):
                qbuf[j, i * block:(i + 1) * block, :] = queries[:, i * HDIM:(i + 1) * HDIM]

    def attend(layer, src, first):
        key_tile = kv[layer, src, :, 0].reshape(split * block, HDIM)
        value_tile = kv[layer, src, :, 1].reshape(split * block, HDIM)

        def rows(j, carry):
            scores = lax.dot_general(
                qbuf[j], key_tile, (((1,), (1,)), ((), ())), preferred_element_type=jnp.float32
            )
            own = order_ref[z * split + j]
            own_doc = doc_ref[own]
            parts = []
            for b in range(split):
                other = order_ref[src * split + b]
                limit = jnp.where(doc_ref[other] == own_doc, (own - other) * block, -(1 << 24))
                bias = jnp.where(diff <= limit, 0.0, NEG)
                part = scores[:, b * block:(b + 1) * block].reshape(REP, block, block)
                parts.append((part * factor + bias[None]).reshape(REP * block, block))
            top = functools.reduce(jnp.maximum, parts)
            top = jnp.max(top, axis=1, keepdims=True)
            if not first:
                old = mbuf[j]
                top = jnp.maximum(old, top)
            else:
                top = jnp.broadcast_to(top, (REP * block, 128))
            expo = [jnp.exp2(part - top) for part in parts]
            added = functools.reduce(jnp.add, expo)
            weights = jnp.concatenate([e.astype(jnp.bfloat16) for e in expo], axis=1)
            product = jnp.dot(weights, value_tile, preferred_element_type=jnp.float32)
            mbuf[j] = top
            if first:
                lbuf[j] = added
                acc[j] = product
            else:
                shrink = jnp.exp2(old - top)
                lbuf[j] = lbuf[j] * shrink + added
                acc[j] = acc[j] * shrink + product
            return carry

        lax.fori_loop(0, split, rows, 0, unroll=True)

    def o_copy(layer, j):
        return remote(
            obuf.at[layer, j], rbuf.at[k],
            o_send.at[layer, j], o_recv.at[k], (layer, z * split + j),
        )

    def o_local(layer, j):
        return pltpu.make_async_copy(
            obuf.at[layer, j], out_ref.at[0, :, cols(k, QW)], o_send.at[layer, j]
        )

    def finish(layer):
        for j in range(split):
            wide = (hbuf[j] if layer == 0 else obuf[layer - 1, j]).astype(jnp.float32)
            total = jnp.sum(lbuf[j], axis=1, keepdims=True)
            attended = (acc[j] / total).astype(jnp.bfloat16).astype(jnp.float32)
            for i in range(REP):
                span = slice(i * HDIM, (i + 1) * HDIM)
                obuf[layer, j, :, span] = (
                    wide[:, span] + attended[i * block:(i + 1) * block]
                ).astype(jnp.bfloat16)
            mine = (p == layer) & (g == j)

            @pl.when(mine)
            def _():
                o_local(layer, j).start()

            @pl.when(jnp.logical_not(mine))
            def _():
                o_copy(layer, j).start()

    def send_next(layer, t):
        if layer + 1 == layers:
            return

        @pl.when(z == t)
        def _():
            for b in range(split):
                send_chunk(layer + 1, z, b, True)

        @pl.when(groups - 1 - z == t)
        def _():
            for b in range(split):
                send_chunk(layer + 1, z, b, False)

    for layer in range(layers):
        make_queries(layer)
        attend(layer, z, True)
        if layer == 0:
            for later in range(1, layers):
                for b in range(split):
                    wait_chunk(later, b)
        send_next(layer, 0)

        def step(t, carry):
            below, above = z - t, z + t

            @pl.when(below >= 0)
            def _():
                for b in range(split):
                    z_copy(layer, below, b, True).wait_recv()
                    send_chunk(layer, below, b, True)

            @pl.when(above < groups)
            def _():
                for b in range(split):
                    z_copy(layer, above, b, False).wait_recv()
                    send_chunk(layer, above, b, False)

            send_next(layer, t)

            @pl.when(below >= 0)
            def _():
                attend(layer, below, False)

            @pl.when(above < groups)
            def _():
                attend(layer, above, False)

            return carry

        lax.fori_loop(1, groups, step, 0)
        finish(layer)

    for i in range(1, KVH):
        kv_copy(i).wait_send()
    for i in range(1, split):
        e_copy(i).wait_send()
    for i in range(1, layers):
        g_copy(i).wait_send()
    for layer in range(layers):
        for i in range(1, KVH):
            s_copy(layer, i).wait_send()

        def drain(src, carry):
            @pl.when((src <= z) & (z < groups - 1))
            def _():
                for b in range(split):
                    z_copy(layer, src, b, True).wait_send()

            @pl.when((src >= z) & (z > 0))
            def _():
                for b in range(split):
                    z_copy(layer, src, b, False).wait_send()

            return carry

        lax.fori_loop(0, groups, drain, 0)
        for j in range(split):
            mine = (p == layer) & (g == j)

            @pl.when(mine)
            def _():
                o_local(layer, j).wait()

            @pl.when(jnp.logical_not(mine))
            def _():
                o_copy(layer, j).wait_send()

    def place(i):
        return pltpu.make_async_copy(
            rbuf.at[peer(i)], out_ref.at[0, :, cols(peer(i), QW)], r_sem.at[i]
        )

    for i in range(1, KVH):
        spot = rbuf.at[peer(i)]
        remote(spot, spot, o_send.at[0, 0], o_recv.at[peer(i)], (p, c)).wait_recv()
        place(i).start()
    for i in range(1, KVH):
        place(i).wait()


def body(layers, ctx, embed, gains, keys, values, block_order, block_doc):
    block, width = embed.shape
    split = KVH // layers
    groups = ctx // split
    dma = pltpu.SemaphoreType.DMA
    smem = pl.BlockSpec(memory_space=pltpu.SMEM)
    anywhere = pl.BlockSpec(memory_space=pl.ANY)
    rows = REP * block
    return pl.pallas_call(
        functools.partial(kernel, layers, ctx, block),
        out_shape=jax.ShapeDtypeStruct((1, block, width), jnp.bfloat16),
        in_specs=[smem, smem] + [anywhere] * 4,
        out_specs=anywhere,
        scratch_shapes=[
            pltpu.VMEM((layers, groups, split, 2, block, HDIM), jnp.bfloat16),
            pltpu.VMEM((split, block, QW), jnp.bfloat16),
            pltpu.VMEM((layers, 1, QW), jnp.float32),
            pltpu.VMEM((layers, split, block, QW), jnp.bfloat16),
            pltpu.VMEM((split, rows, HDIM), jnp.bfloat16),
            pltpu.VMEM((split, rows, 128), jnp.float32),
            pltpu.VMEM((split, rows, 128), jnp.float32),
            pltpu.VMEM((split, rows, HDIM), jnp.float32),
            pltpu.VMEM((layers, 8, 128), jnp.float32),
            pltpu.VMEM((layers, KVH, 8, 128), jnp.float32),
            pltpu.VMEM((KVH, 2, block, HDIM), jnp.bfloat16),
            pltpu.VMEM((split, block, QW), jnp.bfloat16),
            pltpu.VMEM((KVH, block, QW), jnp.bfloat16),
            dma((4,)),
            dma((KVH,)),
            dma((layers, split)),
            dma((split,)),
            dma((split,)),
            dma((layers,)),
            dma((layers,)),
            dma((layers, KVH)),
            dma((layers, KVH)),
            dma((layers, groups, 2, split)),
            dma((layers, groups, split)),
            dma((layers, split)),
            dma((KVH,)),
            dma((KVH, 2)),
            dma((split,)),
            dma((KVH,)),
        ],
        compiler_params=pltpu.CompilerParams(
            collective_id=0, has_side_effects=True, vmem_limit_bytes=48 * 1024 * 1024
        ),
    )(block_order, block_doc, embed, gains, keys, values)


def solution(mesh):
    placed = (
        P("ctx", None),
        P("phase", None),
        P("phase", "ctx", None),
        P("phase", "ctx", None),
        P(),
        P(),
    )
    run = functools.partial(body, mesh.shape["phase"], mesh.shape["ctx"])
    return jax.shard_map(
        run, mesh=mesh, in_specs=placed, out_specs=P("phase", "ctx", None), check_vma=False
    )
```

```python
import functools
import math

import jax
import jax.numpy as jnp
from jax import lax
from jax.experimental import pallas as pl
from jax.experimental.pallas import tpu as pltpu
from jax.sharding import PartitionSpec as P

HEADS = 32
KVH = 8
HDIM = 128
REP = HEADS // KVH
QW = REP * HDIM
NEG = -1e30
MESH = pl.DeviceIdType.MESH


def kernel(
    layers, ctx, block,
    order_ref, doc_ref, embed_ref, gains_ref, keys_ref, values_ref,
    out_ref,
    kv, hbuf, gbuf, obuf, qbuf, mbuf, lbuf, acc, ss_send, ss_recv, kst, est, rbuf,
    loc_sem, kv_send, kv_recv, e_send, e_recv, g_send, g_recv,
    s_send, s_recv, z_send, z_recv, o_send, o_recv, st_sem, e_st_sem, r_sem,
):
    split = KVH // layers
    groups = ctx // split
    p = lax.axis_index("phase")
    c = lax.axis_index("ctx")
    g = lax.rem(c, split)
    z = lax.div(c, split)
    k = p * split + g
    width = embed_ref.shape[1]

    def device_of(head, group):
        return (lax.div(head, split), group * split + lax.rem(head, split))

    def peer(i):
        return lax.rem(k + i, KVH)

    barrier = pltpu.get_barrier_semaphore()
    for i in range(1, KVH):
        pl.semaphore_signal(barrier, inc=1, device_id=device_of(peer(i), z), device_id_type=MESH)

    @pl.when(z > 0)
    def _():
        pl.semaphore_signal(barrier, inc=1, device_id=(p, c - split), device_id_type=MESH)

    @pl.when(z < groups - 1)
    def _():
        pl.semaphore_signal(barrier, inc=1, device_id=(p, c + split), device_id_type=MESH)

    count = KVH - 1 + (z > 0).astype(jnp.int32) + (z < groups - 1).astype(jnp.int32)
    pl.semaphore_wait(barrier, count)

    def cols(head, size):
        return pl.ds(pl.multiple_of(head * size, size), size)

    def remote(src, dst, send, recv, device):
        return pltpu.make_async_remote_copy(
            src_ref=src, dst_ref=dst, send_sem=send, recv_sem=recv,
            device_id=device, device_id_type=MESH,
        )

    def kv_stage(i, which):
        source = (keys_ref, values_ref)[which]
        return pltpu.make_async_copy(
            source.at[0, :, cols(peer(i), HDIM)], kst.at[i, which], st_sem.at[i, which]
        )

    def kv_copy(i):
        return remote(
            kst.at[i], kv.at[p, z, g], kv_send.at[i], kv_recv.at[p, g], device_of(peer(i), z)
        )

    def kv_arrive(layer, b):
        spot = kv.at[layer, z, b]
        return remote(spot, spot, kv_send.at[0], kv_recv.at[layer, b], (p, c))

    def e_stage(i):
        other = lax.rem(g + i, split)
        return pltpu.make_async_copy(
            embed_ref.at[:, cols(p * split + other, QW)], est.at[i], e_st_sem.at[i]
        )

    def e_copy(i):
        other = lax.rem(g + i, split)
        return remote(est.at[i], hbuf.at[g], e_send.at[i], e_recv.at[g], (p, z * split + other))

    def g_copy(i):
        other = lax.rem(p + i, layers)
        return remote(
            gains_ref.at[:, cols(other * split + g, QW)], gbuf.at[p],
            g_send.at[i], g_recv.at[p], (other, c),
        )

    locals_ = [
        pltpu.make_async_copy(keys_ref.at[0, :, cols(k, HDIM)], kv.at[p, z, g, 0], loc_sem.at[0]),
        pltpu.make_async_copy(values_ref.at[0, :, cols(k, HDIM)], kv.at[p, z, g, 1], loc_sem.at[1]),
        pltpu.make_async_copy(embed_ref.at[:, cols(k, QW)], hbuf.at[g], loc_sem.at[2]),
        pltpu.make_async_copy(gains_ref.at[:, cols(k, QW)], gbuf.at[p], loc_sem.at[3]),
    ]
    for copy in locals_:
        copy.start()
    for i in range(1, KVH):
        kv_stage(i, 0).start()
        kv_stage(i, 1).start()
    for i in range(1, split):
        e_stage(i).start()
    for i in range(1, KVH):
        kv_stage(i, 0).wait()
        kv_stage(i, 1).wait()
        kv_copy(i).start()
    for i in range(1, split):
        e_stage(i).wait()
        e_copy(i).start()
    for i in range(1, layers):
        g_copy(i).start()
    for copy in locals_:
        copy.wait()

    def z_copy(layer, src, b, up):
        spot = kv.at[layer, src, b]
        step = split if up else -split
        return remote(
            spot, spot, z_send.at[layer, src, int(up), b], z_recv.at[layer, src, b], (p, c + step)
        )

    def wait_chunk(layer, b):
        @pl.when(jnp.logical_not((p == layer) & (g == b)))
        def _():
            kv_arrive(layer, b).wait_recv()

    def send_chunk(layer, src, b, up):
        @pl.when(z < groups - 1 if up else z > 0)
        def _():
            z_copy(layer, src, b, up).start()

    for i in range(split):
        b = lax.rem(g + i, split)
        wait_chunk(0, b)
        send_chunk(0, z, b, True)
        send_chunk(0, z, b, False)

    for i in range(1, split):
        b = lax.rem(g + i, split)
        remote(hbuf.at[b], hbuf.at[b], e_send.at[0], e_recv.at[b], (p, c)).wait_recv()
    for i in range(1, layers):
        other = lax.rem(p + i, layers)
        remote(gbuf.at[other], gbuf.at[other], g_send.at[0], g_recv.at[other], (p, c)).wait_recv()

    lane = lax.broadcasted_iota(jnp.int32, (block, 128), 1)
    diff = lane - lax.broadcasted_iota(jnp.int32, (block, 128), 0)
    factor = math.log2(math.e) / math.sqrt(HDIM)

    def s_copy(layer, i):
        return remote(
            ss_send.at[layer], ss_recv.at[layer, k],
            s_send.at[layer, i], s_recv.at[layer, k], device_of(peer(i), z),
        )

    def make_queries(layer):
        def hidden(j):
            return (hbuf[j] if layer == 0 else obuf[layer - 1, j]).astype(jnp.float32)

        partial = jnp.zeros((block, 128), jnp.float32)
        for j in range(split):
            wide = hidden(j)
            partial = jnp.where(lane == j, jnp.sum(wide * wide, axis=1, keepdims=True), partial)
        turned = partial.T[:8]
        ss_send[layer] = turned
        ss_recv[layer, k] = turned
        for i in range(1, KVH):
            s_copy(layer, i).start()
        for i in range(1, KVH):
            other = peer(i)
            spot = ss_recv.at[layer, other]
            remote(spot, spot, s_send.at[layer, 0], s_recv.at[layer, other], (p, c)).wait_recv()
        total = jnp.sum(ss_recv[layer], axis=0)
        scale = lax.rsqrt(total * (1.0 / width) + 1e-05)
        scale = jnp.concatenate([scale] * (block // 8), axis=0).T
        for j in range(split):
            queries = (hidden(j) * scale[:, j:j + 1] * gbuf[layer]).astype(jnp.bfloat16)
            for i in range(REP):
                qbuf[j, i * block:(i + 1) * block, :] = queries[:, i * HDIM:(i + 1) * HDIM]

    def attend(layer, src, first, last=False):
        key_tile = kv[layer, src, :, 0].reshape(split * block, HDIM)
        value_tile = kv[layer, src, :, 1].reshape(split * block, HDIM)

        def rows(j):
            scores = lax.dot_general(
                qbuf[j], key_tile, (((1,), (1,)), ((), ())), preferred_element_type=jnp.float32
            )
            own = order_ref[z * split + j]
            own_doc = doc_ref[own]
            parts = []
            for b in range(split):
                other = order_ref[src * split + b]
                limit = jnp.where(doc_ref[other] == own_doc, (own - other) * block, -(1 << 24))
                bias = jnp.where(diff <= limit, 0.0, NEG)
                part = scores[:, b * block:(b + 1) * block].reshape(REP, block, block)
                parts.append((part * factor + bias[None]).reshape(REP * block, block))
            top = functools.reduce(jnp.maximum, parts)
            top = jnp.max(top, axis=1, keepdims=True)
            if not first:
                old = mbuf[j]
                top = jnp.maximum(old, top)
            else:
                top = jnp.broadcast_to(top, (REP * block, 128))
            expo = [jnp.exp2(part - top) for part in parts]
            added = functools.reduce(jnp.add, expo)
            weights = jnp.concatenate([e.astype(jnp.bfloat16) for e in expo], axis=1)
            product = jnp.dot(weights, value_tile, preferred_element_type=jnp.float32)
            mbuf[j] = top
            if first:
                lbuf[j] = added
                acc[j] = product
            else:
                shrink = jnp.exp2(old - top)
                lbuf[j] = lbuf[j] * shrink + added
                acc[j] = acc[j] * shrink + product

        for i in range(split):
            j = lax.rem(g + 1 + i, split)
            rows(j)
            if last:
                finish(layer, j, i == split - 1)

    def o_copy(layer, j):
        return remote(
            obuf.at[layer, j], rbuf.at[k],
            o_send.at[layer, j], o_recv.at[k], (layer, z * split + j),
        )

    def o_local(layer, j):
        return pltpu.make_async_copy(
            obuf.at[layer, j], out_ref.at[0, :, cols(k, QW)], o_send.at[layer, j]
        )

    def finish(layer, j, at_home):
        wide = (hbuf[j] if layer == 0 else obuf[layer - 1, j]).astype(jnp.float32)
        total = jnp.sum(lbuf[j], axis=1, keepdims=True)
        attended = (acc[j] / total).astype(jnp.bfloat16).astype(jnp.float32)
        for i in range(REP):
            span = slice(i * HDIM, (i + 1) * HDIM)
            obuf[layer, j, :, span] = (
                wide[:, span] + attended[i * block:(i + 1) * block]
            ).astype(jnp.bfloat16)
        if at_home:
            @pl.when(p == layer)
            def _():
                o_local(layer, j).start()

            @pl.when(p != layer)
            def _():
                o_copy(layer, j).start()
        else:
            o_copy(layer, j).start()

    def send_next(layer, t):
        if layer + 1 == layers:
            return

        @pl.when(z == t)
        def _():
            for b in range(split):
                send_chunk(layer + 1, z, b, True)

        @pl.when(groups - 1 - z == t)
        def _():
            for b in range(split):
                send_chunk(layer + 1, z, b, False)

    for layer in range(layers):
        make_queries(layer)
        attend(layer, z, True, groups == 1)
        if layer == 0:
            for later in range(1, layers):
                for b in range(split):
                    wait_chunk(later, b)
        send_next(layer, 0)

        def step(t, carry):
            below, above = z - t, z + t

            @pl.when(below >= 0)
            def _():
                for b in range(split):
                    z_copy(layer, below, b, True).wait_recv()
                    send_chunk(layer, below, b, True)

            @pl.when(above < groups)
            def _():
                for b in range(split):
                    z_copy(layer, above, b, False).wait_recv()
                    send_chunk(layer, above, b, False)

            send_next(layer, t)

            ends = t == jnp.maximum(z, groups - 1 - z)
            ends_below = ends & (above >= groups)

            @pl.when((below >= 0) & jnp.logical_not(ends_below))
            def _():
                attend(layer, below, False)

            @pl.when((above < groups) & jnp.logical_not(ends))
            def _():
                attend(layer, above, False)

            @pl.when(ends)
            def _():
                attend(layer, jnp.where(above < groups, above, below), False, True)

            return carry

        lax.fori_loop(1, groups, step, 0)

    for i in range(1, KVH):
        kv_copy(i).wait_send()
    for i in range(1, split):
        e_copy(i).wait_send()
    for i in range(1, layers):
        g_copy(i).wait_send()
    for layer in range(layers):
        for i in range(1, KVH):
            s_copy(layer, i).wait_send()

        def drain(src, carry):
            @pl.when((src <= z) & (z < groups - 1))
            def _():
                for b in range(split):
                    z_copy(layer, src, b, True).wait_send()

            @pl.when((src >= z) & (z > 0))
            def _():
                for b in range(split):
                    z_copy(layer, src, b, False).wait_send()

            return carry

        lax.fori_loop(0, groups, drain, 0)
        for j in range(split):
            mine = (p == layer) & (g == j)

            @pl.when(mine)
            def _():
                o_local(layer, j).wait()

            @pl.when(jnp.logical_not(mine))
            def _():
                o_copy(layer, j).wait_send()

    def place(i):
        return pltpu.make_async_copy(
            rbuf.at[peer(i)], out_ref.at[0, :, cols(peer(i), QW)], r_sem.at[i]
        )

    for i in range(1, KVH):
        spot = rbuf.at[peer(i)]
        remote(spot, spot, o_send.at[0, 0], o_recv.at[peer(i)], (p, c)).wait_recv()
        place(i).start()
    for i in range(1, KVH):
        place(i).wait()


def body(layers, ctx, embed, gains, keys, values, block_order, block_doc):
    block, width = embed.shape
    split = KVH // layers
    groups = ctx // split
    dma = pltpu.SemaphoreType.DMA
    smem = pl.BlockSpec(memory_space=pltpu.SMEM)
    anywhere = pl.BlockSpec(memory_space=pl.ANY)
    rows = REP * block
    return pl.pallas_call(
        functools.partial(kernel, layers, ctx, block),
        out_shape=jax.ShapeDtypeStruct((1, block, width), jnp.bfloat16),
        in_specs=[smem, smem] + [anywhere] * 4,
        out_specs=anywhere,
        scratch_shapes=[
            pltpu.VMEM((layers, groups, split, 2, block, HDIM), jnp.bfloat16),
            pltpu.VMEM((split, block, QW), jnp.bfloat16),
            pltpu.VMEM((layers, 1, QW), jnp.float32),
            pltpu.VMEM((layers, split, block, QW), jnp.bfloat16),
            pltpu.VMEM((split, rows, HDIM), jnp.bfloat16),
            pltpu.VMEM((split, rows, 128), jnp.float32),
            pltpu.VMEM((split, rows, 128), jnp.float32),
            pltpu.VMEM((split, rows, HDIM), jnp.float32),
            pltpu.VMEM((layers, 8, 128), jnp.float32),
            pltpu.VMEM((layers, KVH, 8, 128), jnp.float32),
            pltpu.VMEM((KVH, 2, block, HDIM), jnp.bfloat16),
            pltpu.VMEM((split, block, QW), jnp.bfloat16),
            pltpu.VMEM((KVH, block, QW), jnp.bfloat16),
            dma((4,)),
            dma((KVH,)),
            dma((layers, split)),
            dma((split,)),
            dma((split,)),
            dma((layers,)),
            dma((layers,)),
            dma((layers, KVH)),
            dma((layers, KVH)),
            dma((layers, groups, 2, split)),
            dma((layers, groups, split)),
            dma((layers, split)),
            dma((KVH,)),
            dma((KVH, 2)),
            dma((split,)),
            dma((KVH,)),
        ],
        compiler_params=pltpu.CompilerParams(
            collective_id=0, has_side_effects=True, vmem_limit_bytes=48 * 1024 * 1024
        ),
    )(block_order, block_doc, embed, gains, keys, values)


def solution(mesh):
    placed = (
        P("ctx", None),
        P("phase", None),
        P("phase", "ctx", None),
        P("phase", "ctx", None),
        P(),
        P(),
    )
    run = functools.partial(body, mesh.shape["phase"], mesh.shape["ctx"])
    return jax.shard_map(
        run, mesh=mesh, in_specs=placed, out_specs=P("phase", "ctx", None), check_vma=False
    )
```

```python
import functools
import math

import jax
import jax.numpy as jnp
from jax import lax
from jax.experimental import pallas as pl
from jax.experimental.pallas import tpu as pltpu
from jax.sharding import PartitionSpec as P

HEADS = 32
KVH = 8
HDIM = 128
REP = HEADS // KVH
QW = REP * HDIM
NEG = -1e30
MESH = pl.DeviceIdType.MESH


def kernel(
    layers, ctx, block,
    order_ref, doc_ref, embed_ref, gains_ref, keys_ref, values_ref,
    out_ref,
    kv, hbuf, gbuf, obuf, qbuf, mbuf, lbuf, acc, ss_send, ss_recv, kst, est, rbuf,
    loc_sem, kv_send, kv_recv, e_send, e_recv, g_send, g_recv,
    s_send, s_recv, z_send, z_recv, o_send, o_recv, st_sem, e_st_sem, r_sem,
):
    split = KVH // layers
    groups = ctx // split
    p = lax.axis_index("phase")
    c = lax.axis_index("ctx")
    g = lax.rem(c, split)
    z = lax.div(c, split)
    k = p * split + g
    width = embed_ref.shape[1]

    def device_of(head, group):
        return (lax.div(head, split), group * split + lax.rem(head, split))

    def peer(i):
        return lax.rem(k + i, KVH)

    barrier = pltpu.get_barrier_semaphore()
    for i in range(1, KVH):
        pl.semaphore_signal(barrier, inc=1, device_id=device_of(peer(i), z), device_id_type=MESH)

    @pl.when(z > 0)
    def _():
        pl.semaphore_signal(barrier, inc=1, device_id=(p, c - split), device_id_type=MESH)

    @pl.when(z < groups - 1)
    def _():
        pl.semaphore_signal(barrier, inc=1, device_id=(p, c + split), device_id_type=MESH)

    count = KVH - 1 + (z > 0).astype(jnp.int32) + (z < groups - 1).astype(jnp.int32)
    pl.semaphore_wait(barrier, count)

    def cols(head, size):
        return pl.ds(pl.multiple_of(head * size, size), size)

    def remote(src, dst, send, recv, device):
        return pltpu.make_async_remote_copy(
            src_ref=src, dst_ref=dst, send_sem=send, recv_sem=recv,
            device_id=device, device_id_type=MESH,
        )

    def kv_stage(i, which):
        source = (keys_ref, values_ref)[which]
        return pltpu.make_async_copy(
            source.at[0, :, cols(peer(i), HDIM)], kst.at[i, which], st_sem.at[i, which]
        )

    def kv_copy(i):
        return remote(
            kst.at[i], kv.at[p, z, g], kv_send.at[i], kv_recv.at[p, g], device_of(peer(i), z)
        )

    def kv_arrive(layer, b):
        spot = kv.at[layer, z, b]
        return remote(spot, spot, kv_send.at[0], kv_recv.at[layer, b], (p, c))

    def e_stage(i):
        other = lax.rem(g + i, split)
        return pltpu.make_async_copy(
            embed_ref.at[:, cols(p * split + other, QW)], est.at[i], e_st_sem.at[i]
        )

    def e_copy(i):
        other = lax.rem(g + i, split)
        return remote(est.at[i], hbuf.at[g], e_send.at[i], e_recv.at[g], (p, z * split + other))

    def g_copy(i):
        other = lax.rem(p + i, layers)
        return remote(
            gains_ref.at[:, cols(other * split + g, QW)], gbuf.at[p],
            g_send.at[i], g_recv.at[p], (other, c),
        )

    locals_ = [
        pltpu.make_async_copy(keys_ref.at[0, :, cols(k, HDIM)], kv.at[p, z, g, 0], loc_sem.at[0]),
        pltpu.make_async_copy(values_ref.at[0, :, cols(k, HDIM)], kv.at[p, z, g, 1], loc_sem.at[1]),
        pltpu.make_async_copy(embed_ref.at[:, cols(k, QW)], hbuf.at[g], loc_sem.at[2]),
        pltpu.make_async_copy(gains_ref.at[:, cols(k, QW)], gbuf.at[p], loc_sem.at[3]),
    ]
    for copy in locals_:
        copy.start()
    for i in range(1, KVH):
        kv_stage(i, 0).start()
        kv_stage(i, 1).start()
    for i in range(1, split):
        e_stage(i).start()
    for i in range(1, KVH):
        kv_stage(i, 0).wait()
        kv_stage(i, 1).wait()
        kv_copy(i).start()
    for i in range(1, split):
        e_stage(i).wait()
        e_copy(i).start()
    for i in range(1, layers):
        g_copy(i).start()
    for copy in locals_:
        copy.wait()

    def z_copy(layer, src, b, up):
        spot = kv.at[layer, src, b]
        step = split if up else -split
        return remote(
            spot, spot, z_send.at[layer, src, int(up), b], z_recv.at[layer, src, b], (p, c + step)
        )

    def wait_chunk(layer, b):
        @pl.when(jnp.logical_not((p == layer) & (g == b)))
        def _():
            kv_arrive(layer, b).wait_recv()

    def send_chunk(layer, src, b, up):
        @pl.when(z < groups - 1 if up else z > 0)
        def _():
            z_copy(layer, src, b, up).start()

    for i in range(split):
        b = lax.rem(g + i, split)
        wait_chunk(0, b)
        send_chunk(0, z, b, True)
        send_chunk(0, z, b, False)

    for i in range(1, split):
        b = lax.rem(g + i, split)
        remote(hbuf.at[b], hbuf.at[b], e_send.at[0], e_recv.at[b], (p, c)).wait_recv()
    for i in range(1, layers):
        other = lax.rem(p + i, layers)
        remote(gbuf.at[other], gbuf.at[other], g_send.at[0], g_recv.at[other], (p, c)).wait_recv()

    lane = lax.broadcasted_iota(jnp.int32, (block, 128), 1)
    diff = lane - lax.broadcasted_iota(jnp.int32, (block, 128), 0)
    factor = math.log2(math.e) / math.sqrt(HDIM)

    def s_copy(layer, i):
        return remote(
            ss_send.at[layer], ss_recv.at[layer, k],
            s_send.at[layer, i], s_recv.at[layer, k], device_of(peer(i), z),
        )

    def make_queries(layer):
        def hidden(j):
            return (hbuf[j] if layer == 0 else obuf[layer - 1, j]).astype(jnp.float32)

        partial = jnp.zeros((block, 128), jnp.float32)
        for j in range(split):
            wide = hidden(j)
            partial = jnp.where(lane == j, jnp.sum(wide * wide, axis=1, keepdims=True), partial)
        turned = partial.T[:8]
        ss_send[layer] = turned
        ss_recv[layer, k] = turned
        for i in range(1, KVH):
            s_copy(layer, i).start()
        for i in range(1, KVH):
            other = peer(i)
            spot = ss_recv.at[layer, other]
            remote(spot, spot, s_send.at[layer, 0], s_recv.at[layer, other], (p, c)).wait_recv()
        total = jnp.sum(ss_recv[layer], axis=0)
        scale = lax.rsqrt(total * (1.0 / width) + 1e-05)
        scale = jnp.concatenate([scale] * (block // 8), axis=0).T
        for j in range(split):
            queries = (hidden(j) * scale[:, j:j + 1] * gbuf[layer]).astype(jnp.bfloat16)
            for i in range(REP):
                qbuf[j, i * block:(i + 1) * block, :] = queries[:, i * HDIM:(i + 1) * HDIM]

    def attend(layer, src, first, last=False):
        key_tile = kv[layer, src, :, 0].reshape(split * block, HDIM)
        value_tile = kv[layer, src, :, 1].reshape(split * block, HDIM)

        def rows(j):
            scores = lax.dot_general(
                qbuf[j], key_tile, (((1,), (1,)), ((), ())), preferred_element_type=jnp.float32
            )
            own = order_ref[z * split + j]
            own_doc = doc_ref[own]
            parts = []
            for b in range(split):
                other = order_ref[src * split + b]
                limit = jnp.where(doc_ref[other] == own_doc, (own - other) * block, -(1 << 24))
                bias = jnp.where(diff <= limit, 0.0, NEG)
                part = scores[:, b * block:(b + 1) * block].reshape(REP, block, block)
                parts.append((part * factor + bias[None]).reshape(REP * block, block))
            top = functools.reduce(jnp.maximum, parts)
            top = jnp.max(top, axis=1, keepdims=True)
            if not first:
                old = mbuf[j]
                top = jnp.maximum(old, top)
            else:
                top = jnp.broadcast_to(top, (REP * block, 128))
            expo = [jnp.exp2(part - top) for part in parts]
            added = functools.reduce(jnp.add, expo)
            weights = jnp.concatenate([e.astype(jnp.bfloat16) for e in expo], axis=1)
            product = jnp.dot(weights, value_tile, preferred_element_type=jnp.float32)
            mbuf[j] = top
            if first:
                lbuf[j] = added
                acc[j] = product
            else:
                shrink = jnp.exp2(old - top)
                lbuf[j] = lbuf[j] * shrink + added
                acc[j] = acc[j] * shrink + product

        for i in range(split):
            j = lax.rem(g + 1 + i, split)
            rows(j)
            if last:
                finish(layer, j, i == split - 1)

    def o_copy(layer, j):
        return remote(
            obuf.at[layer, j], rbuf.at[k],
            o_send.at[layer, j], o_recv.at[k], (layer, z * split + j),
        )

    def o_local(layer, j):
        return pltpu.make_async_copy(
            obuf.at[layer, j], out_ref.at[0, :, cols(k, QW)], o_send.at[layer, j]
        )

    def finish(layer, j, at_home):
        wide = (hbuf[j] if layer == 0 else obuf[layer - 1, j]).astype(jnp.float32)
        total = jnp.sum(lbuf[j], axis=1, keepdims=True)
        attended = (acc[j] / total).astype(jnp.bfloat16).astype(jnp.float32)
        for i in range(REP):
            span = slice(i * HDIM, (i + 1) * HDIM)
            obuf[layer, j, :, span] = (
                wide[:, span] + attended[i * block:(i + 1) * block]
            ).astype(jnp.bfloat16)
        if at_home:
            @pl.when(p == layer)
            def _():
                o_local(layer, j).start()

            @pl.when(p != layer)
            def _():
                o_copy(layer, j).start()
        else:
            o_copy(layer, j).start()

    def send_next(layer, t):
        if layer + 1 == layers:
            return

        @pl.when(z == t)
        def _():
            for b in range(split):
                send_chunk(layer + 1, z, b, True)

        @pl.when(groups - 1 - z == t)
        def _():
            for b in range(split):
                send_chunk(layer + 1, z, b, False)

    def forward(layer, t):
        below, above = z - t, z + t

        @pl.when(below >= 0)
        def _():
            for b in range(split):
                z_copy(layer, below, b, True).wait_recv()
                send_chunk(layer, below, b, True)

        @pl.when(above < groups)
        def _():
            for b in range(split):
                z_copy(layer, above, b, False).wait_recv()
                send_chunk(layer, above, b, False)

        send_next(layer, t)

    for layer in range(layers):
        if layer > 0:
            send_next(layer, 0)
            forward(layer, 1)
        make_queries(layer)
        attend(layer, z, True, groups == 1)
        if layer == 0:
            for later in range(1, layers):
                for b in range(split):
                    wait_chunk(later, b)
            send_next(layer, 0)

        def step(t, carry):
            below, above = z - t, z + t

            @pl.when(t > (0 if layer == 0 else 1))
            def _():
                forward(layer, t)

            ends = t == jnp.maximum(z, groups - 1 - z)
            ends_below = ends & (above >= groups)

            @pl.when((below >= 0) & jnp.logical_not(ends_below))
            def _():
                attend(layer, below, False)

            @pl.when((above < groups) & jnp.logical_not(ends))
            def _():
                attend(layer, above, False)

            @pl.when(ends)
            def _():
                attend(layer, jnp.where(above < groups, above, below), False, True)

            return carry

        lax.fori_loop(1, groups, step, 0)

    for i in range(1, KVH):
        kv_copy(i).wait_send()
    for i in range(1, split):
        e_copy(i).wait_send()
    for i in range(1, layers):
        g_copy(i).wait_send()
    for layer in range(layers):
        for i in range(1, KVH):
            s_copy(layer, i).wait_send()

        def drain(src, carry):
            @pl.when((src <= z) & (z < groups - 1))
            def _():
                for b in range(split):
                    z_copy(layer, src, b, True).wait_send()

            @pl.when((src >= z) & (z > 0))
            def _():
                for b in range(split):
                    z_copy(layer, src, b, False).wait_send()

            return carry

        lax.fori_loop(0, groups, drain, 0)
        for j in range(split):
            mine = (p == layer) & (g == j)

            @pl.when(mine)
            def _():
                o_local(layer, j).wait()

            @pl.when(jnp.logical_not(mine))
            def _():
                o_copy(layer, j).wait_send()

    def place(i):
        return pltpu.make_async_copy(
            rbuf.at[peer(i)], out_ref.at[0, :, cols(peer(i), QW)], r_sem.at[i]
        )

    for i in range(1, KVH):
        spot = rbuf.at[peer(i)]
        remote(spot, spot, o_send.at[0, 0], o_recv.at[peer(i)], (p, c)).wait_recv()
        place(i).start()
    for i in range(1, KVH):
        place(i).wait()


def body(layers, ctx, embed, gains, keys, values, block_order, block_doc):
    block, width = embed.shape
    split = KVH // layers
    groups = ctx // split
    dma = pltpu.SemaphoreType.DMA
    smem = pl.BlockSpec(memory_space=pltpu.SMEM)
    anywhere = pl.BlockSpec(memory_space=pl.ANY)
    rows = REP * block
    return pl.pallas_call(
        functools.partial(kernel, layers, ctx, block),
        out_shape=jax.ShapeDtypeStruct((1, block, width), jnp.bfloat16),
        in_specs=[smem, smem] + [anywhere] * 4,
        out_specs=anywhere,
        scratch_shapes=[
            pltpu.VMEM((layers, groups, split, 2, block, HDIM), jnp.bfloat16),
            pltpu.VMEM((split, block, QW), jnp.bfloat16),
            pltpu.VMEM((layers, 1, QW), jnp.float32),
            pltpu.VMEM((layers, split, block, QW), jnp.bfloat16),
            pltpu.VMEM((split, rows, HDIM), jnp.bfloat16),
            pltpu.VMEM((split, rows, 128), jnp.float32),
            pltpu.VMEM((split, rows, 128), jnp.float32),
            pltpu.VMEM((split, rows, HDIM), jnp.float32),
            pltpu.VMEM((layers, 8, 128), jnp.float32),
            pltpu.VMEM((layers, KVH, 8, 128), jnp.float32),
            pltpu.VMEM((KVH, 2, block, HDIM), jnp.bfloat16),
            pltpu.VMEM((split, block, QW), jnp.bfloat16),
            pltpu.VMEM((KVH, block, QW), jnp.bfloat16),
            dma((4,)),
            dma((KVH,)),
            dma((layers, split)),
            dma((split,)),
            dma((split,)),
            dma((layers,)),
            dma((layers,)),
            dma((layers, KVH)),
            dma((layers, KVH)),
            dma((layers, groups, 2, split)),
            dma((layers, groups, split)),
            dma((layers, split)),
            dma((KVH,)),
            dma((KVH, 2)),
            dma((split,)),
            dma((KVH,)),
        ],
        compiler_params=pltpu.CompilerParams(
            collective_id=0, has_side_effects=True, vmem_limit_bytes=48 * 1024 * 1024
        ),
    )(block_order, block_doc, embed, gains, keys, values)


def solution(mesh):
    placed = (
        P("ctx", None),
        P("phase", None),
        P("phase", "ctx", None),
        P("phase", "ctx", None),
        P(),
        P(),
    )
    run = functools.partial(body, mesh.shape["phase"], mesh.shape["ctx"])
    return jax.shard_map(
        run, mesh=mesh, in_specs=placed, out_specs=P("phase", "ctx", None), check_vma=False
    )
```
